32 devices in a mesh: dp: 4 (over y, x), segment: 4 (over z), chan: 2 (over core).
Axes of the slice: x: 2, y: 2, z: 4, core: 2. Of those that a mesh axis runs over, the one named last changes fastest.
Arguments:
- x_input: bfloat16 [4, 4, 256, 1024], P(None, 'dp', None, 'chan'), may hold values from -48 to 48
- d_output: bfloat16 [4, 4, 256, 1024], P(None, 'dp', None, 'chan'), may hold values from -6 to 6
- weights: bfloat16 [4, 9, 1024, 1024], P('segment', None, None, 'chan'), may hold values from -0.0625 to 0.0625
- gains: float32 [4, 1024], P('segment', 'chan'), may hold values from 0.5 to 1.5
- biases: float32 [4, 1024], P('segment', 'chan'), may hold values from -3 to 3
Outputs:
- d_weights: float32 [4, 9, 1024, 1024], P('segment', None, None, 'chan')
- d_gains: float32 [4, 1024], P('segment', 'chan')
- d_biases: float32 [4, 1024], P('segment', 'chan')
The draws below stay inside these ranges and needn't reach their ends.
All inputs are finite; a program needn't handle non-finite values.
Results may differ from the reference program's by a relative error of at most 0.025.
Values may be sent and summed in bfloat16 or wider, within the bound.
A program may use at most 128 MiB of HBM per device.

```python
import jax
import jax.numpy as jnp
from jax import lax

C = 1024
GROUPS = 32
SIDE = 16
MICRO = 4
IMAGES = 4
SECTIONS = 4
N_CHAN = 2


def draw_x_input(key, part):
    key_base, key_chan, key_pixel = jax.random.split(key, 3)
    base_values = jax.random.truncated_normal(key_base, -4.0, 4.0, (MICRO, IMAGES, SIDE * SIDE, C), jnp.float32)
    chan_scale = jnp.exp(jax.random.uniform(key_chan, (C,), jnp.float32, jnp.log(0.5), jnp.log(5.0)))
    pixel_scale = jnp.exp(jax.random.uniform(key_pixel, (MICRO, IMAGES, SIDE * SIDE, 1), jnp.float32, jnp.log(0.5), jnp.log(2.0)))
    values = base_values * chan_scale * pixel_scale
    return values.astype(jnp.bfloat16)


def levels(key, dims, cuts, smallest, largest):
    factor_of, own = 1.0, jax.random.fold_in(key, 6)
    for dim, shards_of in cuts:
        heights = jnp.exp(jax.random.uniform(jax.random.fold_in(own, dim), (shards_of,), jnp.float32, smallest / len(cuts), largest / len(cuts)))
        factor_of = factor_of * jnp.repeat(heights, dims[dim] // shards_of).reshape([-1 if axis == dim else 1 for axis in range(len(dims))])
    return factor_of


def scatter_about(stream_key, shape, width, bound, cuts=(), held_as=jnp.bfloat16):
    entries = width * jax.random.normal(stream_key, shape, jnp.float32)
    if cuts:
        entries = entries * levels(stream_key, shape, cuts, -0.22, 0.18)
    return jnp.clip(entries, -bound, bound).astype(held_as)


def setup_inputs(seed: int = 0) -> dict:
    arg_keys = jax.random.split(jax.random.key(seed), 6)
    return {
        "x_input": draw_x_input(jax.random.fold_in(arg_keys[5], 71), 0),
        "d_output": scatter_about(arg_keys[1], (MICRO, IMAGES, SIDE * SIDE, C), 1.0, 6.0, ((1, 4), (3, 2))),
        "weights": scatter_about(arg_keys[2], (SECTIONS, 9, C, C), (9 * C) ** -0.5, 0.0625, ((0, 4), (3, 2))),
        "gains": jnp.clip(1.0 + 0.1 * jax.random.normal(arg_keys[3], (SECTIONS, C), jnp.float32), 0.5, 1.5),
        "biases": scatter_about(arg_keys[4], (SECTIONS, C), 0.5, 3.0, ((0, 4), (1, 2)), jnp.float32),
    }


EPSILON = 1e-05

def expand_groups(statistic, channels):
    return jnp.repeat(statistic, channels // GROUPS, axis=1)[:, None, :]

def group_means(values):
    batch_count, pixel_count, channels = values.shape
    grouped = values.reshape(batch_count, pixel_count, GROUPS, channels // GROUPS)
    return lax.optimization_barrier(jnp.mean(grouped, axis=(1, 3)))

def shifted_stack(images, forward_taps):
    batch_count, pixel_count, channels = images.shape
    square = images.reshape(batch_count, SIDE, SIDE, channels)
    padded = jnp.pad(square, ((0, 0), (1, 1), (1, 1), (0, 0)))
    tap_list = []
    for tap_y in range(3):
        for tap_x in range(3):
            start_y = tap_y if forward_taps else 2 - tap_y
            start_x = tap_x if forward_taps else 2 - tap_x
            window = padded[:, start_y:start_y + SIDE, start_x:start_x + SIDE, :]
            tap_list.append(window.reshape(batch_count * pixel_count, channels))
    return jnp.stack(tap_list)

def block_forward(inputs, weight, gain_row, bias_row):
    values = inputs.astype(jnp.float32)
    group_mean = group_means(values)
    centred = values - expand_groups(group_mean, C)
    group_rstd = lax.rsqrt(group_means(centred * centred) + EPSILON)
    normed = centred * expand_groups(group_rstd, C)
    pre_act = normed * gain_row + bias_row
    hidden = (pre_act * jax.nn.sigmoid(pre_act)).astype(jnp.bfloat16)
    tap_stack = shifted_stack(hidden, True).astype(jnp.float32)
    conv_out = jnp.einsum('trc,tco->ro', tap_stack, weight.astype(jnp.float32), precision=lax.Precision.HIGHEST)
    output = (values + conv_out.reshape(values.shape)).astype(jnp.bfloat16)
    return (output, (inputs, group_mean, group_rstd))

def block_backward(grad_out, saved, weight, gain_row, bias_row):
    inputs, group_mean, group_rstd = saved
    values = inputs.astype(jnp.float32)
    normed = (values - expand_groups(group_mean, C)) * expand_groups(group_rstd, C)
    pre_act = normed * gain_row + bias_row
    sigma = jax.nn.sigmoid(pre_act)
    hidden = (pre_act * sigma).astype(jnp.bfloat16)
    grad_rows = grad_out.reshape(-1, C).astype(jnp.float32)
    grad_weight = jnp.einsum('trc,ro->tco', shifted_stack(hidden, True).astype(jnp.float32), grad_rows, precision=lax.Precision.HIGHEST)
    back_stack = shifted_stack(grad_out, False).astype(jnp.float32)
    row_total = back_stack.shape[1]
    block_width = C // N_CHAN
    back_blocks = back_stack.reshape(9, row_total, N_CHAN, block_width)
    weight_blocks = weight.astype(jnp.float32).reshape(9, C, N_CHAN, block_width)
    partials = jnp.einsum('trkp,tckp->krc', back_blocks, weight_blocks, precision=lax.Precision.HIGHEST)
    partials = partials.astype(jnp.bfloat16).astype(jnp.float32)
    grad_hidden = lax.optimization_barrier(jnp.sum(partials, axis=0)).reshape(values.shape)
    grad_pre = grad_hidden * sigma * (1.0 + pre_act * (1.0 - sigma))
    grad_gain = lax.optimization_barrier(jnp.sum(grad_pre * normed, axis=(0, 1)))
    grad_bias = lax.optimization_barrier(jnp.sum(grad_pre, axis=(0, 1)))
    grad_normed = grad_pre * gain_row
    first_mean = group_means(grad_normed)
    second_mean = group_means(grad_normed * normed)
    grad_in = grad_out.astype(jnp.float32) + expand_groups(group_rstd, C) * (grad_normed - expand_groups(first_mean, C) - normed * expand_groups(second_mean, C))
    return (grad_in.astype(jnp.bfloat16), grad_weight, grad_gain, grad_bias)

def reference(x_input, d_output, weights, gains, biases):
    sections = weights.shape[0]
    half_way = sections // 2
    weight_sums = [jnp.zeros((9, C, C), jnp.float32) for section in range(sections)]
    gain_sums = [jnp.zeros((C,), jnp.float32) for section in range(sections)]
    bias_sums = [jnp.zeros((C,), jnp.float32) for section in range(sections)]
    for micro_index in range(MICRO):
        saved_list = [None] * sections
        skip_list = []
        current = x_input[micro_index]
        for section in range(half_way):
            current, saved_list[section] = block_forward(current, weights[section], gains[section], biases[section])
            skip_list.append(current)
        upward = jnp.zeros_like(current)
        for branch in reversed(range(half_way)):
            joined = (upward.astype(jnp.float32) + skip_list[branch].astype(jnp.float32)).astype(jnp.bfloat16)
            section = 2 * half_way - 1 - branch
            upward, saved_list[section] = block_forward(joined, weights[section], gains[section], biases[section])
        grad_now = d_output[micro_index]
        skip_grads = []
        for branch in range(half_way):
            section = 2 * half_way - 1 - branch
            grad_now, grad_weight, grad_gain, grad_bias = block_backward(grad_now, saved_list[section], weights[section], gains[section], biases[section])
            weight_sums[section] = weight_sums[section] + grad_weight
            gain_sums[section] = gain_sums[section] + grad_gain
            bias_sums[section] = bias_sums[section] + grad_bias
            skip_grads.append(grad_now)
        later_grad = None
        for section in reversed(range(half_way)):
            if section == half_way - 1:
                grad_now = skip_grads[section]
            else:
                grad_now = (skip_grads[section].astype(jnp.float32) + later_grad.astype(jnp.float32)).astype(jnp.bfloat16)
            later_grad, grad_weight, grad_gain, grad_bias = block_backward(grad_now, saved_list[section], weights[section], gains[section], biases[section])
            weight_sums[section] = weight_sums[section] + grad_weight
            gain_sums[section] = gain_sums[section] + grad_gain
            bias_sums[section] = bias_sums[section] + grad_bias
    return (jnp.stack(weight_sums), jnp.stack(gain_sums), jnp.stack(bias_sums))
```

```python
import functools

import jax
import jax.numpy as jnp
from jax import lax
from jax.experimental import pallas as pl
from jax.experimental.pallas import tpu as pltpu
from jax.sharding import PartitionSpec as P

GROUPS = 32
SIDE = 16
PIXELS = SIDE * SIDE
EPSILON = 1e-05
F32 = jnp.float32
BF16 = jnp.bfloat16
MESH = pl.DeviceIdType.MESH
LIMIT = 60 * 1024 * 1024


def row_sums(values):
    return jnp.sum(values.reshape(-1, 8, values.shape[1]), axis=0)


def group_spread(partial, group_width):
    width = partial.shape[1]
    total = jnp.broadcast_to(jnp.sum(partial, axis=0, keepdims=True), partial.shape)
    lane = lax.broadcasted_iota(jnp.int32, partial.shape, 1)
    step = 1
    while step < group_width:
        above = pltpu.roll(total, width - step, 1)
        below = pltpu.roll(total, step, 1)
        total = total + jnp.where((lane & step) != 0, below, above)
        step *= 2
    return total[0:1]


def fill_shifts(dst, piece, offset, stride, forward):
    width = piece.shape[1]
    values = piece.astype(F32)
    column = lax.broadcasted_iota(jnp.int32, (PIXELS, width), 0) % SIDE
    for tap_x in range(3):
        by = tap_x - 1 if forward else 1 - tap_x
        if by == 0:
            moved = piece
        elif by == 1:
            moved = jnp.where(column < SIDE - 1, pltpu.roll(values, PIXELS - 1, 0), 0.0).astype(BF16)
        else:
            moved = jnp.where(column > 0, pltpu.roll(values, 1, 0), 0.0).astype(BF16)
        start = pl.multiple_of(tap_x * stride + offset, 128)
        dst[SIDE : SIDE + PIXELS, pl.ds(start, width)] = moved


def pipeline_kernel(
    segments, chans, copies, micros, group_width,
    x_ref, dout_ref, w_ref, gain_ref, bias_ref,
    hall, dyall, dgain_ref, dbias_ref,
    fin, yout, bin_, bout, abuf, mean_buf, rstd_buf, hx, dyx, psend, precv, stat,
    fs_send, fs_recv, bs_send, bs_recv, hc_send, hc_recv, hd_send, hd_recv,
    hf_send, hf_recv, dd_send, dd_recv, pc_send, pc_recv, st_send, st_recv,
):
    half = segments // 2
    p = lax.axis_index("segment")
    me = lax.axis_index("chan")
    img = lax.axis_index("dp")
    width = w_ref.shape[2]
    full = w_ref.shape[1]
    count = float(PIXELS * group_width)
    own = pl.ds(pl.multiple_of(me * width, 128), width)

    def chan_peer(r):
        return lax.rem(me + r, chans)

    def dp_peer(r):
        return lax.rem(img + r, copies)

    barrier = pltpu.get_barrier_semaphore()

    def greet(where):
        pl.semaphore_signal(barrier, inc=1, device_id=where, device_id_type=MESH)

    for r in range(1, chans):
        greet({"chan": chan_peer(r)})
    for r in range(1, copies):
        greet({"dp": dp_peer(r)})

    @pl.when(p > 0)
    def _():
        greet({"segment": p - 1})

    @pl.when(p < segments - 1)
    def _():
        greet({"segment": p + 1})

    neighbours = (p > 0).astype(jnp.int32) + (p < segments - 1).astype(jnp.int32)
    pl.semaphore_wait(barrier, chans - 1 + copies - 1 + neighbours)

    hx[0:SIDE, :] = jnp.zeros((SIDE, hx.shape[1]), BF16)
    hx[SIDE + PIXELS :, :] = jnp.zeros((SIDE, hx.shape[1]), BF16)
    dyx[0:SIDE, :] = jnp.zeros((SIDE, dyx.shape[1]), BF16)
    dyx[SIDE + PIXELS :, :] = jnp.zeros((SIDE, dyx.shape[1]), BF16)
    stat[img] = jnp.zeros(stat.shape[1:], F32)

    def remote(src, dst, send, recv, where):
        return pltpu.make_async_remote_copy(
            src_ref=src, dst_ref=dst, send_sem=send, recv_sem=recv,
            device_id=where, device_id_type=MESH,
        )

    class Lane:
        def __init__(self, q, by, slots, outs, send, recv):
            self.q, self.slots, self.outs, self.send, self.recv = q, slots, outs, send, recv
            self.to = {"segment": jnp.clip(p + by, 0, segments - 1)}
            self.early = q < half
            self.lev = segments - 1 - q
            self.in_slot = jnp.where(self.early, jnp.maximum(q - 1, 0), self.lev)
            self.lower = jnp.maximum(self.lev - 1, 0)
            self.low_slot = jnp.minimum(self.lower, half - 1)
            self.out_slot = jnp.where(self.early, q, self.low_slot)
            self.arrive = jnp.where(self.early, q, self.lev + 1)
            self.onward = jnp.where(self.early, q, self.lower)
            self.sends = q < segments - 1

        def pass_on(self, m, k):
            slot = self.slots.at[m, k]
            return remote(slot, slot, self.send.at[m, k], self.recv.at[m, k], self.to)

        def put(self, m):
            return remote(
                self.outs.at[m], self.slots.at[m, self.out_slot],
                self.send.at[m, self.out_slot], self.recv.at[m, self.out_slot], self.to,
            )

        def take(self, m):
            for k in range(half):
                @pl.when(k < self.arrive)
                def _():
                    self.pass_on(m, k).wait_recv()

                @pl.when(k < self.onward)
                def _():
                    self.pass_on(m, k).start()

        def give(self, m, value):
            @pl.when(self.sends)
            def _():
                @pl.when(self.early)
                def _():
                    self.outs[m] = value

                @pl.when(jnp.logical_not(self.early))
                def _():
                    skip = self.slots[m, self.low_slot].astype(F32)
                    self.outs[m] = (value.astype(F32) + skip).astype(BF16)

                self.put(m).start()

        def finish(self, m):
            @pl.when(self.sends)
            def _():
                self.put(m).wait_send()

            for k in range(half):
                @pl.when(k < self.onward)
                def _():
                    self.pass_on(m, k).wait_send()

    up = Lane(p, 1, fin, yout, fs_send, fs_recv)
    back = Lane(segments - 1 - p, -1, bin_, bout, bs_send, bs_recv)

    def h_chan(m, r):
        piece = hall.at[m, img, :, own]
        return remote(piece, piece, hc_send.at[m, r], hc_recv.at[m, r], {"chan": chan_peer(r)})

    def h_dp(m, r):
        piece = hall.at[m, img, :, own]
        return remote(piece, piece, hd_send.at[m, r], hd_recv.at[m, r], {"dp": dp_peer(r)})

    def h_fan(m, r, c):
        piece = hall.at[m, lax.rem(img - r + copies, copies), :, own]
        return remote(piece, piece, hf_send.at[m, r, c], hf_recv.at[m, r, c], {"chan": chan_peer(c)})

    def dy_dp(m, r):
        piece = dyall.at[m, img]
        return remote(piece, piece, dd_send.at[m, r], dd_recv.at[m, r], {"dp": dp_peer(r)})

    def part(m, r):
        return remote(
            psend.at[m, r], precv.at[m, r], pc_send.at[m, r], pc_recv.at[m, r],
            {"chan": chan_peer(r)},
        )

    def forward(m):
        @pl.when(p == 0)
        def _():
            abuf[m] = x_ref[m]

        @pl.when(p > 0)
        def _():
            up.take(m)
            abuf[m] = fin[m, up.in_slot]

        values = abuf[m].astype(F32)
        mean = group_spread(row_sums(values), group_width) / count
        centred = values - mean
        var = group_spread(row_sums(centred * centred), group_width) / count
        rstd = lax.rsqrt(var + EPSILON)
        mean_buf[m] = jnp.broadcast_to(mean, (8, width))
        rstd_buf[m] = jnp.broadcast_to(rstd, (8, width))
        pre = centred * rstd * gain_ref[...] + bias_ref[...]
        hall[m, img, :, own] = (pre * jax.nn.sigmoid(pre)).astype(BF16)
        for r in range(1, chans):
            h_chan(m, r).start()
        for r in range(1, copies):
            h_dp(m, r).start()

        @pl.when(up.sends)
        def _():
            fill_shifts(hx, hall[m, img, :, own], me * width, full, True)

        for r in range(1, chans):
            h_chan(m, r).wait_recv()

            @pl.when(up.sends)
            def _():
                other = lax.rem(me - r + chans, chans) * width
                piece = hall[m, img, :, pl.ds(pl.multiple_of(other, 128), width)]
                fill_shifts(hx, piece, other, full, True)

        @pl.when(up.sends)
        def _():
            acc = abuf[m].astype(F32)
            for tap_y in range(3):
                acc += jnp.dot(
                    hx[tap_y * SIDE : tap_y * SIDE + PIXELS, :],
                    w_ref[3 * tap_y : 3 * tap_y + 3].reshape(3 * full, width),
                    preferred_element_type=F32,
                )
            up.give(m, acc.astype(BF16))

    def backward(m):
        @pl.when(p == segments - 1)
        def _():
            dyall[m, img] = dout_ref[m]

        @pl.when(p < segments - 1)
        def _():
            back.take(m)
            dyall[m, img] = bin_[m, back.in_slot]

        for r in range(1, copies):
            dy_dp(m, r).start()
        fill_shifts(dyx, dyall[m, img], 0, width, False)
        for r in list(range(1, chans)) + [0]:
            rows = pl.ds(pl.multiple_of(chan_peer(r) * width, 128), width)
            acc = jnp.zeros((PIXELS, width), F32)
            for tap_y in range(3):
                for tap_x in range(3):
                    acc += lax.dot_general(
                        dyx[(2 - tap_y) * SIDE : (2 - tap_y) * SIDE + PIXELS,
                            tap_x * width : (tap_x + 1) * width],
                        w_ref[3 * tap_y + tap_x, rows, :],
                        (((1,), (1,)), ((), ())),
                        preferred_element_type=F32,
                    )
            psend[m, r] = acc.astype(BF16)
            if r:
                part(m, r).start()
        grad = psend[m, 0].astype(F32)
        for r in range(1, chans):
            part(m, r).wait_recv()
            grad += precv[m, r].astype(F32)
        rstd = rstd_buf[m][0:1]
        normed = (abuf[m].astype(F32) - mean_buf[m][0:1]) * rstd
        pre = normed * gain_ref[...] + bias_ref[...]
        sigma = jax.nn.sigmoid(pre)
        grad = grad * sigma * (1.0 + pre * (1.0 - sigma))
        stat[img, 0:8] += row_sums(grad * normed)
        stat[img, 8:16] += row_sums(grad)

        @pl.when(back.sends)
        def _():
            scaled = grad * gain_ref[...]
            first = group_spread(row_sums(scaled), group_width) / count
            second = group_spread(row_sums(scaled * normed), group_width) / count
            down = dyall[m, img].astype(F32) + rstd * (scaled - first - normed * second)
            back.give(m, down.astype(BF16))

    lag = segments - 1 - p

    def step(s, carry):
        @pl.when(s < micros)
        def _():
            forward(jnp.minimum(s, micros - 1))

        @pl.when(jnp.logical_and(s >= lag, s < lag + micros))
        def _():
            backward(jnp.clip(s - lag, 0, micros - 1))

        return carry

    lax.fori_loop(0, micros + segments - 1, step, 0)

    def stat_dp(r):
        return remote(stat.at[img], stat.at[img], st_send.at[r], st_recv.at[r], {"dp": dp_peer(r)})

    for r in range(1, copies):
        stat_dp(r).start()

    def spread(m, carry):
        for r in range(1, copies):
            h_dp(m, r).wait_recv()
            for c in range(1, chans):
                h_fan(m, r, c).start()
        return carry

    lax.fori_loop(0, micros, spread, 0)
    for r in range(1, copies):
        stat_dp(r).wait_recv()
    total = stat[0]
    for d in range(1, copies):
        total = total + stat[d]
    dgain_ref[...] = jnp.sum(total[0:8], axis=0, keepdims=True)
    dbias_ref[...] = jnp.sum(total[8:16], axis=0, keepdims=True)

    def drain(m, carry):
        for r in range(1, copies):
            dy_dp(m, r).wait_recv()
            for c in range(1, chans):
                h_fan(m, r, c).wait_recv()
        for r in range(1, copies):
            dy_dp(m, r).wait_send()
            h_dp(m, r).wait_send()
            for c in range(1, chans):
                h_fan(m, r, c).wait_send()
        for r in range(1, chans):
            h_chan(m, r).wait_send()
            part(m, r).wait_send()
        up.finish(m)
        back.finish(m)
        return carry

    lax.fori_loop(0, micros, drain, 0)
    for r in range(1, copies):
        stat_dp(r).wait_send()


def weight_kernel(h_ref, dy_ref, out_ref, ht, dyx):
    micros, copies = h_ref.shape[:2]
    width = dy_ref.shape[3]
    images = micros * copies

    @pl.when(pl.program_id(0) == 0)
    def _():
        def build(i, carry):
            slab = dyx.at[i]
            slab[0:SIDE, :] = jnp.zeros((SIDE, slab.shape[1]), BF16)
            slab[SIDE + PIXELS :, :] = jnp.zeros((SIDE, slab.shape[1]), BF16)
            fill_shifts(slab, dy_ref[i // copies, i % copies], 0, width, False)
            return carry

        lax.fori_loop(0, images, build, 0)

    for i in range(images):
        ht[:, i * PIXELS : (i + 1) * PIXELS] = h_ref[i // copies, i % copies].T
    for tap_y in range(3):
        for tap_x in range(3):
            rows = dyx[:, (2 - tap_y) * SIDE : (2 - tap_y) * SIDE + PIXELS,
                       tap_x * width : (tap_x + 1) * width]
            out_ref[3 * tap_y + tap_x] = jnp.dot(
                ht[...], rows.reshape(images * PIXELS, width), preferred_element_type=F32
            )


def local(segments, chans, copies, x_input, d_output, weights, gains, biases):
    micros, images, pixels, width = x_input.shape
    taps, full = weights.shape[1:3]
    half = segments // 2
    group_width = full // GROUPS
    vmem = pl.BlockSpec(memory_space=pltpu.VMEM)
    dma = pltpu.SemaphoreType.DMA
    act = (pixels, width)
    hall, dyall, dgain, dbias = pl.pallas_call(
        functools.partial(pipeline_kernel, segments, chans, copies, micros, group_width),
        out_shape=[
            jax.ShapeDtypeStruct((micros, copies, pixels, full), BF16),
            jax.ShapeDtypeStruct((micros, copies, pixels, width), BF16),
            jax.ShapeDtypeStruct((1, width), F32),
            jax.ShapeDtypeStruct((1, width), F32),
        ],
        in_specs=[vmem] * 5,
        out_specs=[vmem] * 4,
        scratch_shapes=[
            pltpu.VMEM((micros, half) + act, BF16),
            pltpu.VMEM((micros,) + act, BF16),
            pltpu.VMEM((micros, half) + act, BF16),
            pltpu.VMEM((micros,) + act, BF16),
            pltpu.VMEM((micros,) + act, BF16),
            pltpu.VMEM((micros, 8, width), F32),
            pltpu.VMEM((micros, 8, width), F32),
            pltpu.VMEM((pixels + 2 * SIDE, 3 * full), BF16),
            pltpu.VMEM((pixels + 2 * SIDE, 3 * width), BF16),
            pltpu.VMEM((micros, chans) + act, BF16),
            pltpu.VMEM((micros, chans) + act, BF16),
            pltpu.VMEM((copies, 16, width), F32),
            dma((micros, half)), dma((micros, half)),
            dma((micros, half)), dma((micros, half)),
            dma((micros, chans)), dma((micros, chans)),
            dma((micros, copies)), dma((micros, copies)),
            dma((micros, copies, chans)), dma((micros, copies, chans)),
            dma((micros, copies)), dma((micros, copies)),
            dma((micros, chans)), dma((micros, chans)),
            dma((copies,)), dma((copies,)),
        ],
        compiler_params=pltpu.CompilerParams(
            collective_id=0, has_side_effects=True, vmem_limit_bytes=LIMIT
        ),
        name="pipeline",
    )(
        x_input.reshape(micros, pixels, width),
        d_output.reshape(micros, pixels, width),
        weights[0], gains, biases,
    )
    block = min(256, full)
    dw = pl.pallas_call(
        weight_kernel,
        grid=(full // block,),
        out_shape=jax.ShapeDtypeStruct((taps, full, width), F32),
        in_specs=[
            pl.BlockSpec((micros, copies, pixels, block), lambda i: (0, 0, 0, i)),
            pl.BlockSpec((micros, copies, pixels, width), lambda i: (0, 0, 0, 0)),
        ],
        out_specs=pl.BlockSpec((taps, block, width), lambda i: (0, i, 0)),
        scratch_shapes=[
            pltpu.VMEM((block, micros * copies * pixels), BF16),
            pltpu.VMEM((micros * copies, pixels + 2 * SIDE, 3 * width), BF16),
        ],
        compiler_params=pltpu.CompilerParams(vmem_limit_bytes=LIMIT),
        name="weight_grad",
    )(hall, dyall)
    return (dw[None], dgain, dbias)


def solution(mesh):
    in_specs = (
        P(None, "dp", None, "chan"),
        P(None, "dp", None, "chan"),
        P("segment", None, None, "chan"),
        P("segment", "chan"),
        P("segment", "chan"),
    )
    out_specs = (P("segment", None, None, "chan"), P("segment", "chan"), P("segment", "chan"))
    body = functools.partial(
        local, mesh.shape["segment"], mesh.shape["chan"], mesh.shape["dp"]
    )
    return jax.shard_map(body, mesh=mesh, in_specs=in_specs, out_specs=out_specs, check_vma=False)
```

```python
import functools

import jax
import jax.numpy as jnp
from jax import lax
from jax.experimental import pallas as pl
from jax.experimental.pallas import tpu as pltpu
from jax.sharding import PartitionSpec as P

GROUPS = 32
SIDE = 16
PIXELS = SIDE * SIDE
EPSILON = 1e-05
F32 = jnp.float32
BF16 = jnp.bfloat16
MESH = pl.DeviceIdType.MESH
LIMIT = 62 * 1024 * 1024


def row_sums(values):
    return jnp.sum(values.reshape(-1, 8, values.shape[1]), axis=0)


def group_spread(partial, group_width):
    width = partial.shape[1]
    total = jnp.broadcast_to(jnp.sum(partial, axis=0, keepdims=True), partial.shape)
    lane = lax.broadcasted_iota(jnp.int32, partial.shape, 1)
    step = 1
    while step < group_width:
        above = pltpu.roll(total, width - step, 1)
        below = pltpu.roll(total, step, 1)
        total = total + jnp.where((lane & step) != 0, below, above)
        step *= 2
    return total[0:1]


def fill_shifts(dst, piece, offset, stride, forward):
    width = piece.shape[1]
    values = piece.astype(F32)
    column = lax.broadcasted_iota(jnp.int32, (PIXELS, width), 0) % SIDE
    for tap_x in range(3):
        by = tap_x - 1 if forward else 1 - tap_x
        if by == 0:
            moved = piece
        elif by == 1:
            moved = jnp.where(column < SIDE - 1, pltpu.roll(values, PIXELS - 1, 0), 0.0).astype(BF16)
        else:
            moved = jnp.where(column > 0, pltpu.roll(values, 1, 0), 0.0).astype(BF16)
        start = pl.multiple_of(tap_x * stride + offset, 128)
        dst[SIDE : SIDE + PIXELS, pl.ds(start, width)] = moved


def pipeline_kernel(
    segments, chans, copies, micros, group_width,
    x_ref, dout_ref, w_ref, gain_ref, bias_ref,
    wsum_ref, hlast_ref, dylast_ref, dgain_ref, dbias_ref,
    hall, dyall, wacc, ht, dyall_x, fin, yout, bin_, bout, abuf, mean_buf, rstd_buf, hx, dyx, psend, precv, stat,
    fs_send, fs_recv, bs_send, bs_recv, hc_send, hc_recv, hd_send, hd_recv,
    hf_send, hf_recv, dd_send, dd_recv, pc_send, pc_recv, st_send, st_recv, wcopy, lcopy,
):
    half = segments // 2
    p = lax.axis_index("segment")
    me = lax.axis_index("chan")
    img = lax.axis_index("dp")
    width = w_ref.shape[2]
    full = w_ref.shape[1]
    count = float(PIXELS * group_width)
    own = pl.ds(pl.multiple_of(me * width, 128), width)

    def chan_peer(r):
        return lax.rem(me + r, chans)

    def dp_peer(r):
        return lax.rem(img + r, copies)

    barrier = pltpu.get_barrier_semaphore()

    def greet(where):
        pl.semaphore_signal(barrier, inc=1, device_id=where, device_id_type=MESH)

    for r in range(1, chans):
        greet({"chan": chan_peer(r)})
    for r in range(1, copies):
        greet({"dp": dp_peer(r)})

    @pl.when(p > 0)
    def _():
        greet({"segment": p - 1})

    @pl.when(p < segments - 1)
    def _():
        greet({"segment": p + 1})

    neighbours = (p > 0).astype(jnp.int32) + (p < segments - 1).astype(jnp.int32)
    pl.semaphore_wait(barrier, chans - 1 + copies - 1 + neighbours)

    hx[0:SIDE, :] = jnp.zeros((SIDE, hx.shape[1]), BF16)
    hx[SIDE + PIXELS :, :] = jnp.zeros((SIDE, hx.shape[1]), BF16)
    dyx[0:SIDE, :] = jnp.zeros((SIDE, dyx.shape[1]), BF16)
    dyx[SIDE + PIXELS :, :] = jnp.zeros((SIDE, dyx.shape[1]), BF16)
    for d in range(copies):
        dyall_x[d, 0:SIDE, :] = jnp.zeros((SIDE, dyx.shape[1]), BF16)
        dyall_x[d, SIDE + PIXELS :, :] = jnp.zeros((SIDE, dyx.shape[1]), BF16)
    stat[img] = jnp.zeros(stat.shape[1:], F32)

    def remote(src, dst, send, recv, where):
        return pltpu.make_async_remote_copy(
            src_ref=src, dst_ref=dst, send_sem=send, recv_sem=recv,
            device_id=where, device_id_type=MESH,
        )

    class Lane:
        def __init__(self, q, by, slots, outs, send, recv):
            self.q, self.slots, self.outs, self.send, self.recv = q, slots, outs, send, recv
            self.to = {"segment": jnp.clip(p + by, 0, segments - 1)}
            self.early = q < half
            self.lev = segments - 1 - q
            self.in_slot = jnp.where(self.early, jnp.maximum(q - 1, 0), self.lev)
            self.lower = jnp.maximum(self.lev - 1, 0)
            self.low_slot = jnp.minimum(self.lower, half - 1)
            self.out_slot = jnp.where(self.early, q, self.low_slot)
            self.arrive = jnp.where(self.early, q, self.lev + 1)
            self.onward = jnp.where(self.early, q, self.lower)
            self.sends = q < segments - 1

        def pass_on(self, m, k):
            slot = self.slots.at[m, k]
            return remote(slot, slot, self.send.at[m, k], self.recv.at[m, k], self.to)

        def put(self, m):
            return remote(
                self.outs.at[m], self.slots.at[m, self.out_slot],
                self.send.at[m, self.out_slot], self.recv.at[m, self.out_slot], self.to,
            )

        def take(self, m):
            for k in range(half):
                @pl.when(k < self.arrive)
                def _():
                    self.pass_on(m, k).wait_recv()

                @pl.when(k < self.onward)
                def _():
                    self.pass_on(m, k).start()

        def give(self, m, value):
            @pl.when(self.sends)
            def _():
                @pl.when(self.early)
                def _():
                    self.outs[m] = value

                @pl.when(jnp.logical_not(self.early))
                def _():
                    skip = self.slots[m, self.low_slot].astype(F32)
                    self.outs[m] = (value.astype(F32) + skip).astype(BF16)

                self.put(m).start()

        def finish(self, m):
            @pl.when(self.sends)
            def _():
                self.put(m).wait_send()

            for k in range(half):
                @pl.when(k < self.onward)
                def _():
                    self.pass_on(m, k).wait_send()

    up = Lane(p, 1, fin, yout, fs_send, fs_recv)
    back = Lane(segments - 1 - p, -1, bin_, bout, bs_send, bs_recv)

    def h_chan(m, r):
        piece = hall.at[m, img, :, own]
        return remote(piece, piece, hc_send.at[m, r], hc_recv.at[m, r], {"chan": chan_peer(r)})

    def h_dp(m, r):
        piece = hall.at[m, img, :, own]
        return remote(piece, piece, hd_send.at[m, r], hd_recv.at[m, r], {"dp": dp_peer(r)})

    def h_fan(m, r, c):
        piece = hall.at[m, lax.rem(img - r + copies, copies), :, own]
        return remote(piece, piece, hf_send.at[m, r, c], hf_recv.at[m, r, c], {"chan": chan_peer(c)})

    def dy_dp(m, r):
        piece = dyall.at[m, img]
        return remote(piece, piece, dd_send.at[m, r], dd_recv.at[m, r], {"dp": dp_peer(r)})

    def part(m, r):
        return remote(
            psend.at[m, r], precv.at[m, r - 1], pc_send.at[m, r], pc_recv.at[m, r],
            {"chan": chan_peer(r)},
        )

    def forward(m):
        @pl.when(p == 0)
        def _():
            abuf[m] = x_ref[m]

        @pl.when(p > 0)
        def _():
            up.take(m)
            abuf[m] = fin[m, up.in_slot]

        values = abuf[m].astype(F32)
        mean = group_spread(row_sums(values), group_width) / count
        centred = values - mean
        var = group_spread(row_sums(centred * centred), group_width) / count
        rstd = lax.rsqrt(var + EPSILON)
        mean_buf[m] = jnp.broadcast_to(mean, (8, width))
        rstd_buf[m] = jnp.broadcast_to(rstd, (8, width))
        pre = centred * rstd * gain_ref[...] + bias_ref[...]
        hall[m, img, :, own] = (pre * jax.nn.sigmoid(pre)).astype(BF16)
        for r in range(1, chans):
            h_chan(m, r).start()
        for r in range(1, copies):
            h_dp(m, r).start()

        @pl.when(up.sends)
        def _():
            fill_shifts(hx, hall[m, img, :, own], me * width, full, True)

        for r in range(1, chans):
            h_chan(m, r).wait_recv()

            @pl.when(up.sends)
            def _():
                other = lax.rem(me - r + chans, chans) * width
                piece = hall[m, img, :, pl.ds(pl.multiple_of(other, 128), width)]
                fill_shifts(hx, piece, other, full, True)

        @pl.when(up.sends)
        def _():
            acc = abuf[m].astype(F32)
            for tap_y in range(3):
                acc += jnp.dot(
                    hx[tap_y * SIDE : tap_y * SIDE + PIXELS, :],
                    w_ref[3 * tap_y : 3 * tap_y + 3].reshape(3 * full, width),
                    preferred_element_type=F32,
                )
            up.give(m, acc.astype(BF16))

    def input_partials(m):
        @pl.when(p == segments - 1)
        def _():
            dyall[m, img] = dout_ref[m]

        @pl.when(p < segments - 1)
        def _():
            back.take(m)
            dyall[m, img] = bin_[m, back.in_slot]

        for r in range(1, copies):
            dy_dp(m, r).start()
        fill_shifts(dyx, dyall[m, img], 0, width, False)
        for r in list(range(1, chans)) + [0]:
            rows = pl.ds(pl.multiple_of(chan_peer(r) * width, 128), width)
            acc = jnp.zeros((PIXELS, width), F32)
            for tap_y in range(3):
                for tap_x in range(3):
                    acc += lax.dot_general(
                        dyx[(2 - tap_y) * SIDE : (2 - tap_y) * SIDE + PIXELS,
                            tap_x * width : (tap_x + 1) * width],
                        w_ref[3 * tap_y + tap_x, rows, :],
                        (((1,), (1,)), ((), ())),
                        preferred_element_type=F32,
                    )
            psend[m, r] = acc.astype(BF16)
            if r:
                part(m, r).start()

    def backward(m):
        grad = psend[m, 0].astype(F32)
        for r in range(1, chans):
            part(m, r).wait_recv()
            grad += precv[m, r - 1].astype(F32)
        rstd = rstd_buf[m][0:1]
        normed = (abuf[m].astype(F32) - mean_buf[m][0:1]) * rstd
        pre = normed * gain_ref[...] + bias_ref[...]
        sigma = jax.nn.sigmoid(pre)
        grad = grad * sigma * (1.0 + pre * (1.0 - sigma))
        stat[img, 0:8] += row_sums(grad * normed)
        stat[img, 8:16] += row_sums(grad)

        @pl.when(back.sends)
        def _():
            scaled = grad * gain_ref[...]
            first = group_spread(row_sums(scaled), group_width) / count
            second = group_spread(row_sums(scaled * normed), group_width) / count
            down = dyall[m, img].astype(F32) + rstd * (scaled - first - normed * second)
            back.give(m, down.astype(BF16))

    block = ht.shape[0]

    def gathered(j):
        for r in range(1, copies):
            h_dp(j, r).wait_recv()
            for c in range(1, chans):
                h_fan(j, r, c).start()
        for r in range(1, copies):
            dy_dp(j, r).wait_recv()
            for c in range(1, chans):
                h_fan(j, r, c).wait_recv()

    def weight_part(j):
        gathered(j)

        @pl.when(j == 0)
        def _():
            def clear(t, carry):
                wacc[t] = jnp.zeros(wacc.shape[1:], F32)
                return carry

            lax.fori_loop(0, wacc.shape[0], clear, 0)

        def build(d, carry):
            fill_shifts(dyall_x.at[d], dyall[j, d], 0, width, False)
            return carry

        lax.fori_loop(0, copies, build, 0)

        def rows_of(c, carry):
            first = pl.multiple_of(c * block, block)
            for d in range(copies):
                ht[:, d * PIXELS : (d + 1) * PIXELS] = hall[j, d, :, pl.ds(first, block)].T
            for tap in range(9):
                start = (2 - tap // 3) * SIDE
                lanes = slice((tap % 3) * width, (tap % 3 + 1) * width)
                rows = dyall_x[:, start : start + PIXELS, lanes].reshape(copies * PIXELS, width)
                wacc[tap, pl.ds(first, block), :] += jnp.dot(
                    ht[...], rows, preferred_element_type=F32
                )
            return carry

        lax.fori_loop(0, full // block, rows_of, 0)

        @pl.when(j == micros - 2)
        def _():
            pltpu.make_async_copy(wacc, wsum_ref, wcopy).start()

    lag = segments - 1 - p
    last = p == segments - 1
    start_f = jnp.where(last, micros, 0)
    start_b = jnp.where(last, micros, lag)
    ahead = jnp.where(p == 0, micros - 1, jnp.where(p == 1, 1, 0))
    behind = jnp.where(p == 0, 1, 2)

    def step(s, carry):
        @pl.when(jnp.logical_and(s >= start_f, s < start_f + micros))
        def _():
            forward(jnp.clip(s - start_f, 0, micros - 1))

        early = s - lag - behind
        late = s - steps + ahead
        now_early = jnp.logical_and(early >= 0, early < ahead)
        now_late = jnp.logical_and(late >= ahead, late < micros - 1)

        @pl.when(jnp.logical_or(now_early, now_late))
        def _():
            weight_part(jnp.clip(jnp.where(now_late, late, early), 0, micros - 2))

        @pl.when(jnp.logical_and(s >= lag, s < lag + micros))
        def _():
            input_partials(jnp.clip(s - lag, 0, micros - 1))

        @pl.when(jnp.logical_and(s >= start_b, s < start_b + micros))
        def _():
            backward(jnp.clip(s - start_b, 0, micros - 1))

        return carry

    steps = max(micros + segments - 1, 2 * micros)
    lax.fori_loop(0, steps + micros - 1, step, 0)

    def stat_dp(r):
        return remote(stat.at[img], stat.at[img], st_send.at[r], st_recv.at[r], {"dp": dp_peer(r)})

    for r in range(1, copies):
        stat_dp(r).start()

    gathered(micros - 1)
    h_copy = pltpu.make_async_copy(hall.at[micros - 1], hlast_ref, lcopy.at[0])
    dy_copy = pltpu.make_async_copy(dyall.at[micros - 1], dylast_ref, lcopy.at[1])
    h_copy.start()
    dy_copy.start()
    for r in range(1, copies):
        stat_dp(r).wait_recv()
    total = stat[0]
    for d in range(1, copies):
        total = total + stat[d]
    dgain_ref[...] = jnp.sum(total[0:8], axis=0, keepdims=True)
    dbias_ref[...] = jnp.sum(total[8:16], axis=0, keepdims=True)

    def drain(m, carry):
        for r in range(1, copies):
            dy_dp(m, r).wait_send()
            h_dp(m, r).wait_send()
            for c in range(1, chans):
                h_fan(m, r, c).wait_send()
        for r in range(1, chans):
            h_chan(m, r).wait_send()
            part(m, r).wait_send()
        up.finish(m)
        back.finish(m)
        return carry

    lax.fori_loop(0, micros, drain, 0)
    for r in range(1, copies):
        stat_dp(r).wait_send()
    h_copy.wait()
    dy_copy.wait()
    pltpu.make_async_copy(wacc, wsum_ref, wcopy).wait()


def weight_kernel(sum_ref, h_ref, dy_ref, out_ref, ht, dyx):
    images = h_ref.shape[0]
    width = dy_ref.shape[2]

    @pl.when(pl.program_id(0) == 0)
    def _():
        def build(i, carry):
            slab = dyx.at[i]
            slab[0:SIDE, :] = jnp.zeros((SIDE, slab.shape[1]), BF16)
            slab[SIDE + PIXELS :, :] = jnp.zeros((SIDE, slab.shape[1]), BF16)
            fill_shifts(slab, dy_ref[i], 0, width, False)
            return carry

        lax.fori_loop(0, images, build, 0)

    for i in range(images):
        ht[:, i * PIXELS : (i + 1) * PIXELS] = h_ref[i].T
    for tap in range(9):
        start = (2 - tap // 3) * SIDE
        rows = dyx[:, start : start + PIXELS, (tap % 3) * width : (tap % 3 + 1) * width]
        out_ref[tap] = sum_ref[tap] + jnp.dot(
            ht[...], rows.reshape(images * PIXELS, width), preferred_element_type=F32
        )


def local(segments, chans, copies, x_input, d_output, weights, gains, biases):
    micros, images, pixels, width = x_input.shape
    taps, full = weights.shape[1:3]
    half = segments // 2
    group_width = full // GROUPS
    vmem = pl.BlockSpec(memory_space=pltpu.VMEM)
    dma = pltpu.SemaphoreType.DMA
    act = (pixels, width)
    block = min(256, full)
    hbm = pl.BlockSpec(memory_space=pl.ANY)
    wsum, hlast, dylast, dgain, dbias = pl.pallas_call(
        functools.partial(pipeline_kernel, segments, chans, copies, micros, group_width),
        out_shape=[
            jax.ShapeDtypeStruct((taps, full, width), F32),
            jax.ShapeDtypeStruct((copies, pixels, full), BF16),
            jax.ShapeDtypeStruct((copies, pixels, width), BF16),
            jax.ShapeDtypeStruct((1, width), F32),
            jax.ShapeDtypeStruct((1, width), F32),
        ],
        in_specs=[vmem] * 5,
        out_specs=[hbm] * 3 + [vmem] * 2,
        scratch_shapes=[
            pltpu.VMEM((micros, copies, pixels, full), BF16),
            pltpu.VMEM((micros, copies, pixels, width), BF16),
            pltpu.VMEM((taps, full, width), F32),
            pltpu.VMEM((block, copies * pixels), BF16),
            pltpu.VMEM((copies, pixels + 2 * SIDE, 3 * width), BF16),
            pltpu.VMEM((micros, half) + act, BF16),
            pltpu.VMEM((micros,) + act, BF16),
            pltpu.VMEM((micros, half) + act, BF16),
            pltpu.VMEM((micros,) + act, BF16),
            pltpu.VMEM((micros,) + act, BF16),
            pltpu.VMEM((micros, 8, width), F32),
            pltpu.VMEM((micros, 8, width), F32),
            pltpu.VMEM((pixels + 2 * SIDE, 3 * full), BF16),
            pltpu.VMEM((pixels + 2 * SIDE, 3 * width), BF16),
            pltpu.VMEM((micros, chans) + act, BF16),
            pltpu.VMEM((micros, chans - 1) + act, BF16),
            pltpu.VMEM((copies, 16, width), F32),
            dma((micros, half)), dma((micros, half)),
            dma((micros, half)), dma((micros, half)),
            dma((micros, chans)), dma((micros, chans)),
            dma((micros, copies)), dma((micros, copies)),
            dma((micros, copies, chans)), dma((micros, copies, chans)),
            dma((micros, copies)), dma((micros, copies)),
            dma((micros, chans)), dma((micros, chans)),
            dma((copies,)), dma((copies,)),
            dma, dma((2,)),
        ],
        compiler_params=pltpu.CompilerParams(
            collective_id=0, has_side_effects=True, vmem_limit_bytes=LIMIT
        ),
        name="pipeline",
    )(
        x_input.reshape(micros, pixels, width),
        d_output.reshape(micros, pixels, width),
        weights[0], gains, biases,
    )
    dw = pl.pallas_call(
        weight_kernel,
        grid=(full // block,),
        out_shape=jax.ShapeDtypeStruct((taps, full, width), F32),
        in_specs=[
            pl.BlockSpec((taps, block, width), lambda i: (0, i, 0)),
            pl.BlockSpec((copies, pixels, block), lambda i: (0, 0, i)),
            pl.BlockSpec((copies, pixels, width), lambda i: (0, 0, 0)),
        ],
        out_specs=pl.BlockSpec((taps, block, width), lambda i: (0, i, 0)),
        scratch_shapes=[
            pltpu.VMEM((block, copies * pixels), BF16),
            pltpu.VMEM((copies, pixels + 2 * SIDE, 3 * width), BF16),
        ],
        compiler_params=pltpu.CompilerParams(vmem_limit_bytes=LIMIT),
        name="weight_grad",
    )(wsum, hlast, dylast)
    return (dw[None], dgain, dbias)


def solution(mesh):
    in_specs = (
        P(None, "dp", None, "chan"),
        P(None, "dp", None, "chan"),
        P("segment", None, None, "chan"),
        P("segment", "chan"),
        P("segment", "chan"),
    )
    out_specs = (P("segment", None, None, "chan"), P("segment", "chan"), P("segment", "chan"))
    body = functools.partial(
        local, mesh.shape["segment"], mesh.shape["chan"], mesh.shape["dp"]
    )
    return jax.shard_map(body, mesh=mesh, in_specs=in_specs, out_specs=out_specs, check_vma=False)
```

```python
import functools

import jax
import jax.numpy as jnp
from jax import lax
from jax.experimental import pallas as pl
from jax.experimental.pallas import tpu as pltpu
from jax.sharding import PartitionSpec as P

GROUPS = 32
SIDE = 16
PIXELS = SIDE * SIDE
EPSILON = 1e-05
F32 = jnp.float32
BF16 = jnp.bfloat16
MESH = pl.DeviceIdType.MESH
LIMIT = 62 * 1024 * 1024


def row_sums(values):
    return jnp.sum(values.reshape(-1, 8, values.shape[1]), axis=0)


def group_spread(partial, group_width):
    width = partial.shape[1]
    total = jnp.broadcast_to(jnp.sum(partial, axis=0, keepdims=True), partial.shape)
    lane = lax.broadcasted_iota(jnp.int32, partial.shape, 1)
    step = 1
    while step < group_width:
        above = pltpu.roll(total, width - step, 1)
        below = pltpu.roll(total, step, 1)
        total = total + jnp.where((lane & step) != 0, below, above)
        step *= 2
    return total[0:1]


def fill_shifts(dst, piece, offset, stride, forward):
    width = piece.shape[1]
    values = piece.astype(F32)
    column = lax.broadcasted_iota(jnp.int32, (PIXELS, width), 0) % SIDE
    for tap_x in range(3):
        by = tap_x - 1 if forward else 1 - tap_x
        if by == 0:
            moved = piece
        elif by == 1:
            moved = jnp.where(column < SIDE - 1, pltpu.roll(values, PIXELS - 1, 0), 0.0).astype(BF16)
        else:
            moved = jnp.where(column > 0, pltpu.roll(values, 1, 0), 0.0).astype(BF16)
        start = pl.multiple_of(tap_x * stride + offset, 128)
        dst[SIDE : SIDE + PIXELS, pl.ds(start, width)] = moved


def pipeline_kernel(
    segments, chans, copies, micros, group_width,
    x_ref, dout_ref, w_ref, gain_ref, bias_ref,
    wsum_ref, hlast_ref, dylast_ref, dgain_ref, dbias_ref,
    hall, dyall, wacc, ht, dyall_x, fin, yout, bin_, bout, abuf, mean_buf, rstd_buf, hx, dyx, psend, precv, stat,
    fs_send, fs_recv, bs_send, bs_recv, hc_send, hc_recv, hd_send, hd_recv,
    hf_send, hf_recv, dd_send, dd_recv, pc_send, pc_recv, st_send, st_recv, wcopy, lcopy,
):
    half = segments // 2
    p = lax.axis_index("segment")
    me = lax.axis_index("chan")
    img = lax.axis_index("dp")
    width = w_ref.shape[2]
    full = w_ref.shape[1]
    count = float(PIXELS * group_width)
    own = pl.ds(pl.multiple_of(me * width, 128), width)

    def chan_peer(r):
        return lax.rem(me + r, chans)

    def dp_peer(r):
        return lax.rem(img + r, copies)

    barrier = pltpu.get_barrier_semaphore()

    def greet(where):
        pl.semaphore_signal(barrier, inc=1, device_id=where, device_id_type=MESH)

    for r in range(1, chans):
        greet({"chan": chan_peer(r)})
    for r in range(1, copies):
        greet({"dp": dp_peer(r)})

    @pl.when(p > 0)
    def _():
        greet({"segment": p - 1})

    @pl.when(p < segments - 1)
    def _():
        greet({"segment": p + 1})

    neighbours = (p > 0).astype(jnp.int32) + (p < segments - 1).astype(jnp.int32)
    pl.semaphore_wait(barrier, chans - 1 + copies - 1 + neighbours)

    hx[0:SIDE, :] = jnp.zeros((SIDE, hx.shape[1]), BF16)
    hx[SIDE + PIXELS :, :] = jnp.zeros((SIDE, hx.shape[1]), BF16)
    dyx[0:SIDE, :] = jnp.zeros((SIDE, dyx.shape[1]), BF16)
    dyx[SIDE + PIXELS :, :] = jnp.zeros((SIDE, dyx.shape[1]), BF16)
    for d in range(copies):
        dyall_x[d, 0:SIDE, :] = jnp.zeros((SIDE, dyx.shape[1]), BF16)
        dyall_x[d, SIDE + PIXELS :, :] = jnp.zeros((SIDE, dyx.shape[1]), BF16)
    stat[img] = jnp.zeros(stat.shape[1:], F32)

    def remote(src, dst, send, recv, where):
        return pltpu.make_async_remote_copy(
            src_ref=src, dst_ref=dst, send_sem=send, recv_sem=recv,
            device_id=where, device_id_type=MESH,
        )

    class Lane:
        def __init__(self, q, by, slots, outs, send, recv):
            self.q, self.slots, self.outs, self.send, self.recv = q, slots, outs, send, recv
            self.to = {"segment": jnp.clip(p + by, 0, segments - 1)}
            self.early = q < half
            self.lev = segments - 1 - q
            self.in_slot = jnp.where(self.early, jnp.maximum(q - 1, 0), self.lev)
            self.lower = jnp.maximum(self.lev - 1, 0)
            self.low_slot = jnp.minimum(self.lower, half - 1)
            self.out_slot = jnp.where(self.early, q, self.low_slot)
            self.arrive = jnp.where(self.early, q, self.lev + 1)
            self.onward = jnp.where(self.early, q, self.lower)
            self.sends = q < segments - 1

        def pass_on(self, m, k):
            slot = self.slots.at[m, k]
            return remote(slot, slot, self.send.at[m, k], self.recv.at[m, k], self.to)

        def put(self, m):
            return remote(
                self.outs.at[m], self.slots.at[m, self.out_slot],
                self.send.at[m, self.out_slot], self.recv.at[m, self.out_slot], self.to,
            )

        def take(self, m):
            for k in range(half):
                @pl.when(k < self.arrive)
                def _():
                    self.pass_on(m, k).wait_recv()

                @pl.when(k < self.onward)
                def _():
                    self.pass_on(m, k).start()

        def give(self, m, value):
            @pl.when(self.sends)
            def _():
                @pl.when(self.early)
                def _():
                    self.outs[m] = value

                @pl.when(jnp.logical_not(self.early))
                def _():
                    skip = self.slots[m, self.low_slot].astype(F32)
                    self.outs[m] = (value.astype(F32) + skip).astype(BF16)

                self.put(m).start()

        def finish(self, m):
            @pl.when(self.sends)
            def _():
                self.put(m).wait_send()

            for k in range(half):
                @pl.when(k < self.onward)
                def _():
                    self.pass_on(m, k).wait_send()

    up = Lane(p, 1, fin, yout, fs_send, fs_recv)
    back = Lane(segments - 1 - p, -1, bin_, bout, bs_send, bs_recv)

    def h_chan(m, r):
        piece = hall.at[m, img, :, own]
        return remote(piece, piece, hc_send.at[m, r], hc_recv.at[m, r], {"chan": chan_peer(r)})

    def h_dp(m, r):
        piece = hall.at[m, img, :, own]
        return remote(piece, piece, hd_send.at[m, r], hd_recv.at[m, r], {"dp": dp_peer(r)})

    def h_fan(m, r, c):
        piece = hall.at[m, lax.rem(img - r + copies, copies), :, own]
        return remote(piece, piece, hf_send.at[m, r, c], hf_recv.at[m, r, c], {"chan": chan_peer(c)})

    def dy_dp(m, r):
        piece = dyall.at[m, img]
        return remote(piece, piece, dd_send.at[m, r], dd_recv.at[m, r], {"dp": dp_peer(r)})

    def part(m, r):
        return remote(
            psend.at[m, r], precv.at[m, r - 1], pc_send.at[m, r], pc_recv.at[m, r],
            {"chan": chan_peer(r)},
        )

    def forward(m):
        @pl.when(p == 0)
        def _():
            abuf[m] = x_ref[m]

        @pl.when(p > 0)
        def _():
            up.take(m)
            abuf[m] = fin[m, up.in_slot]

        values = abuf[m].astype(F32)
        mean = group_spread(row_sums(values), group_width) / count
        centred = values - mean
        var = group_spread(row_sums(centred * centred), group_width) / count
        rstd = lax.rsqrt(var + EPSILON)
        mean_buf[m] = jnp.broadcast_to(mean, (8, width))
        rstd_buf[m] = jnp.broadcast_to(rstd, (8, width))
        pre = centred * rstd * gain_ref[...] + bias_ref[...]
        hall[m, img, :, own] = (pre * jax.nn.sigmoid(pre)).astype(BF16)
        for r in range(1, chans):
            h_chan(m, r).start()
        for r in range(1, copies):
            h_dp(m, r).start()

        @pl.when(up.sends)
        def _():
            fill_shifts(hx, hall[m, img, :, own], me * width, full, True)

        for r in range(1, chans):
            h_chan(m, r).wait_recv()

            @pl.when(up.sends)
            def _():
                other = lax.rem(me - r + chans, chans) * width
                piece = hall[m, img, :, pl.ds(pl.multiple_of(other, 128), width)]
                fill_shifts(hx, piece, other, full, True)

        @pl.when(up.sends)
        def _():
            acc = abuf[m].astype(F32)
            for tap_y in range(3):
                acc += jnp.dot(
                    hx[tap_y * SIDE : tap_y * SIDE + PIXELS, :],
                    w_ref[3 * tap_y : 3 * tap_y + 3].reshape(3 * full, width),
                    preferred_element_type=F32,
                )
            up.give(m, acc.astype(BF16))

    def input_partials(m):
        @pl.when(p == segments - 1)
        def _():
            dyall[m, img] = dout_ref[m]

        @pl.when(p < segments - 1)
        def _():
            back.take(m)
            dyall[m, img] = bin_[m, back.in_slot]

        for r in range(1, copies):
            dy_dp(m, r).start()
        fill_shifts(dyx, dyall[m, img], 0, width, False)
        for r in list(range(1, chans)) + [0]:
            rows = pl.ds(pl.multiple_of(chan_peer(r) * width, 128), width)
            acc = jnp.zeros((PIXELS, width), F32)
            for tap_y in range(3):
                for tap_x in range(3):
                    acc += lax.dot_general(
                        dyx[(2 - tap_y) * SIDE : (2 - tap_y) * SIDE + PIXELS,
                            tap_x * width : (tap_x + 1) * width],
                        w_ref[3 * tap_y + tap_x, rows, :],
                        (((1,), (1,)), ((), ())),
                        preferred_element_type=F32,
                    )
            psend[m, r] = acc.astype(BF16)
            if r:
                part(m, r).start()

    def backward(m):
        grad = psend[m, 0].astype(F32)
        for r in range(1, chans):
            part(m, r).wait_recv()
            grad += precv[m, r - 1].astype(F32)
        rstd = rstd_buf[m][0:1]
        normed = (abuf[m].astype(F32) - mean_buf[m][0:1]) * rstd
        pre = normed * gain_ref[...] + bias_ref[...]
        sigma = jax.nn.sigmoid(pre)
        grad = grad * sigma * (1.0 + pre * (1.0 - sigma))
        stat[img, 0:8] += row_sums(grad * normed)
        stat[img, 8:16] += row_sums(grad)

        @pl.when(back.sends)
        def _():
            scaled = grad * gain_ref[...]
            first = group_spread(row_sums(scaled), group_width) / count
            second = group_spread(row_sums(scaled * normed), group_width) / count
            down = dyall[m, img].astype(F32) + rstd * (scaled - first - normed * second)
            back.give(m, down.astype(BF16))

    block = ht.shape[0]

    def gathered(j):
        for r in range(1, copies):
            h_dp(j, r).wait_recv()
            for c in range(1, chans):
                h_fan(j, r, c).start()
        for r in range(1, copies):
            dy_dp(j, r).wait_recv()
            for c in range(1, chans):
                h_fan(j, r, c).wait_recv()

    def weight_part(j):
        gathered(j)

        @pl.when(j == 0)
        def _():
            def clear(t, carry):
                wacc[t] = jnp.zeros(wacc.shape[1:], F32)
                return carry

            lax.fori_loop(0, wacc.shape[0], clear, 0)

        def build(d, carry):
            fill_shifts(dyall_x.at[d], dyall[j, d], 0, width, False)
            return carry

        lax.fori_loop(0, copies, build, 0)

        def rows_of(c, carry):
            first = pl.multiple_of(c * block, block)
            for d in range(copies):
                ht[:, d * PIXELS : (d + 1) * PIXELS] = hall[j, d, :, pl.ds(first, block)].T
            for tap in range(9):
                start = (2 - tap // 3) * SIDE
                lanes = slice((tap % 3) * width, (tap % 3 + 1) * width)
                rows = dyall_x[:, start : start + PIXELS, lanes].reshape(copies * PIXELS, width)
                wacc[tap, pl.ds(first, block), :] += jnp.dot(
                    ht[...], rows, preferred_element_type=F32
                )
            return carry

        lax.fori_loop(0, full // block, rows_of, 0)

        @pl.when(j == micros - 2)
        def _():
            pltpu.make_async_copy(wacc, wsum_ref, wcopy).start()

    lag = segments - 1 - p
    last = p == segments - 1
    start_f = jnp.where(last, micros, 0)
    start_b = jnp.where(last, micros, lag)
    ahead = jnp.where(p == 0, micros - 2, jnp.where(p == 1, 1, 0))
    behind = jnp.where(p == 0, 1, 2)

    def step(s, carry):
        @pl.when(jnp.logical_and(s >= start_f, s < start_f + micros))
        def _():
            forward(jnp.clip(s - start_f, 0, micros - 1))

        early = s - lag - behind
        late = s - steps + ahead
        now_early = jnp.logical_and(early >= 0, early < ahead)
        now_late = jnp.logical_and(late >= ahead, late < micros - 1)

        @pl.when(jnp.logical_or(now_early, now_late))
        def _():
            weight_part(jnp.clip(jnp.where(now_late, late, early), 0, micros - 2))

        @pl.when(jnp.logical_and(s >= lag, s < lag + micros))
        def _():
            input_partials(jnp.clip(s - lag, 0, micros - 1))

        @pl.when(jnp.logical_and(s >= start_b, s < start_b + micros))
        def _():
            backward(jnp.clip(s - start_b, 0, micros - 1))

        return carry

    steps = max(micros + segments - 1, 2 * micros)
    lax.fori_loop(0, steps + micros - 1, step, 0)

    def stat_dp(r):
        return remote(stat.at[img], stat.at[img], st_send.at[r], st_recv.at[r], {"dp": dp_peer(r)})

    for r in range(1, copies):
        stat_dp(r).start()

    gathered(micros - 1)
    h_copy = pltpu.make_async_copy(hall.at[micros - 1], hlast_ref, lcopy.at[0])
    dy_copy = pltpu.make_async_copy(dyall.at[micros - 1], dylast_ref, lcopy.at[1])
    h_copy.start()
    dy_copy.start()
    for r in range(1, copies):
        stat_dp(r).wait_recv()
    total = stat[0]
    for d in range(1, copies):
        total = total + stat[d]
    dgain_ref[...] = jnp.sum(total[0:8], axis=0, keepdims=True)
    dbias_ref[...] = jnp.sum(total[8:16], axis=0, keepdims=True)

    def drain(m, carry):
        for r in range(1, copies):
            dy_dp(m, r).wait_send()
            h_dp(m, r).wait_send()
            for c in range(1, chans):
                h_fan(m, r, c).wait_send()
        for r in range(1, chans):
            h_chan(m, r).wait_send()
            part(m, r).wait_send()
        up.finish(m)
        back.finish(m)
        return carry

    lax.fori_loop(0, micros, drain, 0)
    for r in range(1, copies):
        stat_dp(r).wait_send()
    h_copy.wait()
    dy_copy.wait()
    pltpu.make_async_copy(wacc, wsum_ref, wcopy).wait()


def weight_kernel(sum_ref, h_ref, dy_ref, out_ref, ht, dyx):
    images = h_ref.shape[0]
    width = dy_ref.shape[2]

    @pl.when(pl.program_id(0) == 0)
    def _():
        def build(i, carry):
            slab = dyx.at[i]
            slab[0:SIDE, :] = jnp.zeros((SIDE, slab.shape[1]), BF16)
            slab[SIDE + PIXELS :, :] = jnp.zeros((SIDE, slab.shape[1]), BF16)
            fill_shifts(slab, dy_ref[i], 0, width, False)
            return carry

        lax.fori_loop(0, images, build, 0)

    for i in range(images):
        ht[:, i * PIXELS : (i + 1) * PIXELS] = h_ref[i].T
    for tap in range(9):
        start = (2 - tap // 3) * SIDE
        rows = dyx[:, start : start + PIXELS, (tap % 3) * width : (tap % 3 + 1) * width]
        out_ref[tap] = sum_ref[tap] + jnp.dot(
            ht[...], rows.reshape(images * PIXELS, width), preferred_element_type=F32
        )


def local(segments, chans, copies, x_input, d_output, weights, gains, biases):
    micros, images, pixels, width = x_input.shape
    taps, full = weights.shape[1:3]
    half = segments // 2
    group_width = full // GROUPS
    vmem = pl.BlockSpec(memory_space=pltpu.VMEM)
    dma = pltpu.SemaphoreType.DMA
    act = (pixels, width)
    block = min(256, full)
    hbm = pl.BlockSpec(memory_space=pl.ANY)
    wsum, hlast, dylast, dgain, dbias = pl.pallas_call(
        functools.partial(pipeline_kernel, segments, chans, copies, micros, group_width),
        out_shape=[
            jax.ShapeDtypeStruct((taps, full, width), F32),
            jax.ShapeDtypeStruct((copies, pixels, full), BF16),
            jax.ShapeDtypeStruct((copies, pixels, width), BF16),
            jax.ShapeDtypeStruct((1, width), F32),
            jax.ShapeDtypeStruct((1, width), F32),
        ],
        in_specs=[vmem] * 5,
        out_specs=[hbm] * 3 + [vmem] * 2,
        scratch_shapes=[
            pltpu.VMEM((micros, copies, pixels, full), BF16),
            pltpu.VMEM((micros, copies, pixels, width), BF16),
            pltpu.VMEM((taps, full, width), F32),
            pltpu.VMEM((min(512, full), copies * pixels), BF16),
            pltpu.VMEM((copies, pixels + 2 * SIDE, 3 * width), BF16),
            pltpu.VMEM((micros, half) + act, BF16),
            pltpu.VMEM((micros,) + act, BF16),
            pltpu.VMEM((micros, half) + act, BF16),
            pltpu.VMEM((micros,) + act, BF16),
            pltpu.VMEM((micros,) + act, BF16),
            pltpu.VMEM((micros, 8, width), F32),
            pltpu.VMEM((micros, 8, width), F32),
            pltpu.VMEM((pixels + 2 * SIDE, 3 * full), BF16),
            pltpu.VMEM((pixels + 2 * SIDE, 3 * width), BF16),
            pltpu.VMEM((micros, chans) + act, BF16),
            pltpu.VMEM((micros, chans - 1) + act, BF16),
            pltpu.VMEM((copies, 16, width), F32),
            dma((micros, half)), dma((micros, half)),
            dma((micros, half)), dma((micros, half)),
            dma((micros, chans)), dma((micros, chans)),
            dma((micros, copies)), dma((micros, copies)),
            dma((micros, copies, chans)), dma((micros, copies, chans)),
            dma((micros, copies)), dma((micros, copies)),
            dma((micros, chans)), dma((micros, chans)),
            dma((copies,)), dma((copies,)),
            dma, dma((2,)),
        ],
        compiler_params=pltpu.CompilerParams(
            collective_id=0, has_side_effects=True, vmem_limit_bytes=LIMIT
        ),
        name="pipeline",
    )(
        x_input.reshape(micros, pixels, width),
        d_output.reshape(micros, pixels, width),
        weights[0], gains, biases,
    )
    dw = pl.pallas_call(
        weight_kernel,
        grid=(full // block,),
        out_shape=jax.ShapeDtypeStruct((taps, full, width), F32),
        in_specs=[
            pl.BlockSpec((taps, block, width), lambda i: (0, i, 0)),
            pl.BlockSpec((copies, pixels, block), lambda i: (0, 0, i)),
            pl.BlockSpec((copies, pixels, width), lambda i: (0, 0, 0)),
        ],
        out_specs=pl.BlockSpec((taps, block, width), lambda i: (0, i, 0)),
        scratch_shapes=[
            pltpu.VMEM((block, copies * pixels), BF16),
            pltpu.VMEM((copies, pixels + 2 * SIDE, 3 * width), BF16),
        ],
        compiler_params=pltpu.CompilerParams(vmem_limit_bytes=LIMIT),
        name="weight_grad",
    )(wsum, hlast, dylast)
    return (dw[None], dgain, dbias)


def solution(mesh):
    in_specs = (
        P(None, "dp", None, "chan"),
        P(None, "dp", None, "chan"),
        P("segment", None, None, "chan"),
        P("segment", "chan"),
        P("segment", "chan"),
    )
    out_specs = (P("segment", None, None, "chan"), P("segment", "chan"), P("segment", "chan"))
    body = functools.partial(
        local, mesh.shape["segment"], mesh.shape["chan"], mesh.shape["dp"]
    )
    return jax.shard_map(body, mesh=mesh, in_specs=in_specs, out_specs=out_specs, check_vma=False)
```
